32 devices in a mesh: space: 8 (over y, x, core), tm: 4 (over z).
Axes of the slice: x: 2, y: 2, z: 4, core: 2. Of those that a mesh axis runs over, the one named last changes fastest.
Arguments:
- latents: bfloat16 [16, 16, 240, 320], P('tm', 'space'), may hold values from -6 to 6
- cotangent: bfloat16 [16, 16, 240, 320], P('tm', 'space'), may hold values from -6 to 6
- conv_weight: bfloat16 [3, 3, 320, 320], replicated, may hold values from -0.109375 to 0.109375
- query_weight: bfloat16 [320, 320], replicated, may hold values from -3 to 3
- key_weight: bfloat16 [320, 320], replicated, may hold values from -3 to 3
- value_weight: bfloat16 [320, 320], replicated, may hold values from -0.3125 to 0.3125
- out_weight: bfloat16 [320, 320], replicated, may hold values from -0.3125 to 0.3125
Outputs:
- grad_input: bfloat16 [16, 16, 240, 320], P('tm', 'space')
- grad_conv: float32 [3, 3, 320, 320], replicated
- grad_query: float32 [320, 320], replicated
- grad_key: float32 [320, 320], replicated
- grad_value: float32 [320, 320], replicated
- grad_out: float32 [320, 320], replicated
The draws below stay inside these ranges and needn't reach their ends.
All inputs are finite; a program needn't handle non-finite values.
Results may differ from the reference program's by a relative error of at most 0.011.
The reference program's roundings to bfloat16 on the way (of `hidden`, `prob_low`, `attended`, `out_grad`, `dscore`, `attn_grad` and `hidden_grad`) count: a program that leaves them out, or rounds other values in their place, can miss the bound.
Values may be sent and summed in bfloat16 or wider, within the bound.
A program may use at most 128 MiB of HBM per device.

```python
import jax
import jax.numpy as jnp
from jax import lax

HEAD_DIM = 64
CHANNELS = 320
WIDTH = 240
FRAMES = 16
ROWS = 16


def draw_query_weight(key, part):
    key = jax.random.fold_in(key, 11)
    own = jnp.clip(jax.random.normal(key, (CHANNELS, CHANNELS), jnp.float32), -4.0, 4.0) * CHANNELS ** (-0.5)
    return own.astype(jnp.bfloat16)


def draw_key_weight(key, part):
    key = jax.random.fold_in(key, 23)
    own = jnp.clip(jax.random.normal(key, (CHANNELS, CHANNELS), jnp.float32), -4.0, 4.0) * CHANNELS ** (-0.5)
    return own.astype(jnp.bfloat16)


def steps_of(rng, dims, shards, smallest, high):
    loudness, own = 1.0, jax.random.fold_in(rng, 6)
    for position, parts in shards:
        steps = jnp.exp(jax.random.uniform(jax.random.fold_in(own, position), (parts,), jnp.float32, smallest / len(shards), high / len(shards)))
        loudness = loudness * jnp.repeat(steps, dims[position] // parts).reshape([-1 if axis == position else 1 for axis in range(len(dims))])
    return loudness


def bell_draw(own_key, extent, deviation, reach, cuts=(), held_as=jnp.bfloat16):
    gain = steps_of(own_key, extent, cuts, -0.22, 0.18) if cuts else 1.0
    array = jax.random.normal(own_key, extent, jnp.float32) * deviation * gain
    return jnp.minimum(jnp.maximum(array, -reach), reach).astype(held_as)


def setup_inputs(seed: int = 0) -> dict:
    key_of = jax.random.split(jax.random.key(seed), 8)
    latents = bell_draw(key_of[0], (FRAMES, ROWS, WIDTH, CHANNELS), 1.0, 6.0, ((0, 4), (1, 8)))
    cotangent = bell_draw(key_of[1], (FRAMES, ROWS, WIDTH, CHANNELS), 1.0, 6.0, ((0, 4), (1, 8)))
    conv_weight = bell_draw(key_of[2], (3, 3, CHANNELS, CHANNELS), (9 * CHANNELS) ** -0.5, 0.109375)
    query_weight = draw_query_weight(jax.random.fold_in(key_of[7], 71), 0)
    key_weight = draw_key_weight(jax.random.fold_in(key_of[7], 71), 0)
    value_weight = bell_draw(key_of[5], (CHANNELS, CHANNELS), CHANNELS ** -0.5, 0.3125)
    out_weight = bell_draw(key_of[6], (CHANNELS, CHANNELS), CHANNELS ** -0.5, 0.3125)
    return {"latents": latents, "cotangent": cotangent, "conv_weight": conv_weight, "query_weight": query_weight, "key_weight": key_weight, "value_weight": value_weight, "out_weight": out_weight}


def project(arr, weight):
    shape = arr.shape
    flat = jnp.dot(arr.reshape(-1, shape[-1]), weight, preferred_element_type=jnp.float32)
    return flat.reshape(shape[:-1] + (weight.shape[1],))

def contract(left, right):
    chans = left.shape[-1]
    return jnp.dot(left.reshape(-1, chans).T, right.reshape(-1, right.shape[-1]), preferred_element_type=jnp.float32)

def attend(query_rows, key_rows, value_rows, out_grad):
    frames, pixels, chans = query_rows.shape
    heads = chans // HEAD_DIM
    scale = HEAD_DIM ** (-0.5)

    def split(arr):
        return arr.astype(jnp.float32).reshape(frames, pixels, heads, HEAD_DIM)
    qsplit, ksplit, vsplit, gsplit = (split(query_rows), split(key_rows), split(value_rows), split(out_grad))
    scores = jnp.einsum('fwhd,gwhd->whfg', qsplit, ksplit) * scale
    prob = jax.nn.softmax(scores, axis=-1)
    prob_low = prob.astype(jnp.bfloat16).astype(jnp.float32)
    attended = jnp.einsum('whfg,gwhd->fwhd', prob_low, vsplit).astype(jnp.bfloat16)
    dprob = jnp.einsum('fwhd,gwhd->whfg', gsplit, vsplit)
    dscore = prob * (dprob - lax.optimization_barrier(jnp.sum(prob * dprob, axis=-1, keepdims=True)))
    dscore = (dscore * scale).astype(jnp.bfloat16).astype(jnp.float32)
    query_grad = jnp.einsum('whfg,gwhd->fwhd', dscore, ksplit).astype(jnp.bfloat16)
    key_grad = jnp.einsum('whfg,fwhd->gwhd', dscore, qsplit).astype(jnp.bfloat16)
    value_grad = jnp.einsum('whfg,fwhd->gwhd', prob_low, gsplit).astype(jnp.bfloat16)
    shape = (frames, pixels, chans)
    return (attended.reshape(shape), query_grad.reshape(shape), key_grad.reshape(shape), value_grad.reshape(shape))

def reference(latents, cotangent, conv_weight, query_weight, key_weight, value_weight, out_weight):
    frames, rows, cols, chans = latents.shape
    padded = jnp.pad(latents, ((0, 0), (1, 1), (1, 1), (0, 0)))
    total = latents.astype(jnp.float32)
    for row_off in range(3):
        for col_off in range(3):
            total = total + project(padded[:, row_off:row_off + rows, col_off:col_off + cols], conv_weight[row_off, col_off])
    hidden = total.astype(jnp.bfloat16)
    queries = project(hidden, query_weight).astype(jnp.bfloat16)
    keys_all = project(hidden, key_weight).astype(jnp.bfloat16)
    values_all = project(hidden, value_weight).astype(jnp.bfloat16)
    out_grad = project(cotangent, out_weight.T).astype(jnp.bfloat16)

    def by_row(arr):
        return jnp.moveaxis(arr, 1, 0)

    def one_row(items):
        return attend(items[0], items[1], items[2], items[3])
    results = lax.map(one_row, (by_row(queries), by_row(keys_all), by_row(values_all), by_row(out_grad)))
    attended, query_grad, key_grad, value_grad = [jnp.moveaxis(item, 0, 1) for item in results]
    norm = 1.0 / jnp.sqrt(jnp.float32(frames * rows * cols))
    grad_out = contract(attended, cotangent) * norm
    grad_query = contract(hidden, query_grad) * norm
    grad_key = contract(hidden, key_grad) * norm
    grad_value = contract(hidden, value_grad) * norm
    attn_grad = (project(query_grad, query_weight.T) + project(key_grad, key_weight.T) + project(value_grad, value_weight.T)).astype(jnp.bfloat16)
    hidden_grad = (cotangent.astype(jnp.float32) + attn_grad.astype(jnp.float32)).astype(jnp.bfloat16)
    kernel_rows = []
    for row_off in range(3):
        kernel_cols = []
        for col_off in range(3):
            kernel_cols.append(contract(padded[:, row_off:row_off + rows, col_off:col_off + cols], hidden_grad) * norm)
        kernel_rows.append(jnp.stack(kernel_cols))
    grad_conv = jnp.stack(kernel_rows)
    grad_padded = jnp.pad(hidden_grad, ((0, 0), (1, 1), (1, 1), (0, 0)))
    result = hidden_grad.astype(jnp.float32)
    for row_off in range(3):
        for col_off in range(3):
            piece = grad_padded[:, 2 - row_off:2 - row_off + rows, 2 - col_off:2 - col_off + cols]
            result = result + project(piece, conv_weight[row_off, col_off].T)
    grad_input = result.astype(jnp.bfloat16)
    return (grad_input, grad_conv, grad_query, grad_key, grad_value, grad_out)
```

```python
import functools

import jax
import jax.numpy as jnp
from jax import lax
from jax.experimental import pallas as pl
from jax.experimental.pallas import tpu as pltpu
from jax.sharding import PartitionSpec as P

HEAD_DIM = 64
PIXEL_BLOCK = 8
F32 = jnp.float32
BF16 = jnp.bfloat16
VMEM_BYTES = 50 * 1024 * 1024
MESH = pl.DeviceIdType.MESH


def call(body, out_shape, args, scratch=(), flops=0, **params):
    size = sum(a.size * a.dtype.itemsize for a in args)
    return pl.pallas_call(
        body,
        out_shape=out_shape,
        in_specs=[pl.BlockSpec(memory_space=pltpu.VMEM)] * len(args),
        out_specs=jax.tree.map(lambda _: pl.BlockSpec(memory_space=pltpu.VMEM), out_shape),
        scratch_shapes=list(scratch),
        compiler_params=pltpu.CompilerParams(vmem_limit_bytes=VMEM_BYTES, **params),
        cost_estimate=pl.CostEstimate(flops=flops, bytes_accessed=2 * size, transcendentals=0),
    )(*args)


def shape_of(shape, dtype):
    return jax.ShapeDtypeStruct(shape, dtype)


def dot(left, right, dims=((1,), (0,))):
    return lax.dot_general(left, right, (dims, ((), ())), preferred_element_type=F32)


def shifted(arr, step, rows, cols):
    total = rows * cols
    moved = pltpu.roll(arr, (-step) % total, 0)
    place = lax.broadcasted_iota(jnp.int32, arr.shape, 0)
    edge = None
    for row in range(rows):
        hit = place == (row * cols + (0 if step < 0 else cols - 1))
        edge = hit if edge is None else edge | hit
    return jnp.where(edge, 0.0, moved)


def regroup(parts, groups):
    chans = parts[0].shape[-1]
    cat = jnp.concatenate([part.reshape(-1, PIXEL_BLOCK, chans) for part in parts], axis=1)
    return cat.astype(BF16)


def regroup_kernel(cells_ref, out_ref):
    frames, rows, cols, chans = cells_ref.shape
    real = rows * cols // PIXEL_BLOCK
    parts = [cells_ref[f].reshape(rows * cols, chans).astype(F32) for f in range(frames)]
    out_ref[0:real] = regroup(parts, real)
    if out_ref.shape[0] > real:
        out_ref[real:] = jnp.zeros((out_ref.shape[0] - real,) + out_ref.shape[1:], BF16)


def conv_kernel(grouped, top_ref, cells_ref, bottom_ref, weight_ref, out_ref, ext, *scratch):
    frames, rows, cols, chans = cells_ref.shape

    def one_frame(f, carry):
        ext[0] = top_ref[f]
        ext[1 : rows + 1] = cells_ref[f]
        ext[rows + 1] = bottom_ref[f]
        total = cells_ref[f].reshape(rows * cols, chans).astype(F32)
        for b in range(3):
            part = None
            for a in range(3):
                piece = ext[a : a + rows].reshape(rows * cols, chans)
                prod = dot(piece, weight_ref[3 * a + b])
                part = prod if part is None else part + prod
            total = total + (part if b == 1 else shifted(part, b - 1, rows, cols))
        if grouped:
            scratch[0][f] = total
        else:
            out_ref[f] = total.astype(BF16).reshape(rows, cols, chans)
        return carry

    lax.fori_loop(0, frames, one_frame, 0)
    if grouped:
        real = rows * cols // PIXEL_BLOCK
        out_ref[0:real] = regroup([scratch[0][f] for f in range(frames)], real)
        if out_ref.shape[0] > real:
            out_ref[real:] = jnp.zeros((out_ref.shape[0] - real,) + out_ref.shape[1:], BF16)


def convolve(top, cells, bottom, weight, groups=None):
    frames, rows, cols, chans = cells.shape
    scratch = [pltpu.VMEM((rows + 2, cols, chans), BF16)]
    if groups is None:
        out = shape_of(cells.shape, BF16)
    else:
        out = shape_of((groups, frames * PIXEL_BLOCK, chans), BF16)
        scratch.append(pltpu.VMEM((frames, rows * cols, chans), F32))
    return call(
        functools.partial(conv_kernel, groups is not None),
        out,
        (top, cells, bottom, weight),
        scratch,
        flops=18 * cells.size * chans,
    )


def attend_kernel(
    hid, cot, wq, wk, wv, wot, wqt, wkt, wvt, cols_o, att_o, qg_o, kg_o, vg_o, q_s, k_s, v_s, g_s
):
    sources, groups, span, chans = hid.shape
    heads = chans // HEAD_DIM
    scale = HEAD_DIM ** (-0.5)
    size = sources * span
    flat = groups * span

    def project(t, carry):
        h = hid[t].reshape(flat, chans)
        for ref, w in ((q_s, wq), (k_s, wk), (v_s, wv)):
            ref[t] = dot(h, w[...]).astype(BF16).reshape(groups, span, chans)
        c = cot[t].reshape(flat, chans)
        g_s[t] = dot(c, wot[...]).astype(BF16).reshape(groups, span, chans)
        return carry

    lax.fori_loop(0, sources, project, 0)

    place = lax.broadcasted_iota(jnp.int32, (1, chans), 1)
    head_masks = [
        jnp.where((place >= h * HEAD_DIM) & (place < (h + 1) * HEAD_DIM), 1.0, 0.0).astype(BF16)
        for h in range(heads)
    ]
    left = lax.broadcasted_iota(jnp.int32, (size, size), 0)
    right = lax.broadcasted_iota(jnp.int32, (size, size), 1)
    same = (left & (PIXEL_BLOCK - 1)) == (right & (PIXEL_BLOCK - 1))

    def one_group(g, carry):
        def get(ref):
            return ref[:, g].reshape(size, chans)

        def stack(arr):
            return jnp.concatenate([arr * m for m in head_masks], axis=0)

        q, k, v, og = get(q_s), get(k_s), get(v_s), get(g_s)
        kst, vst = stack(k), stack(v)
        scores = dot(q, kst, ((1,), (1,))) * scale
        dprobs = dot(og, vst, ((1,), (1,)))
        lows, lows_t, grads, grads_t = [], [], [], []
        for h in range(heads):
            block = slice(h * size, (h + 1) * size)
            s = jnp.where(same, scores[:, block], -1e30)
            e = jnp.exp(s - jnp.max(s, axis=1, keepdims=True))
            prob = e / jnp.sum(e, axis=1, keepdims=True)
            dp = dprobs[:, block]
            ds = prob * (dp - jnp.sum(prob * dp, axis=1, keepdims=True)) * scale
            low, grad = prob.astype(BF16), ds.astype(BF16)
            lows.append(low)
            grads.append(grad)
            lows_t.append(low.T)
            grads_t.append(grad.T)
        shape = (sources, span, chans)
        low = jnp.concatenate(lows, axis=1)
        grad = jnp.concatenate(grads, axis=1)
        low_t = jnp.concatenate(lows_t, axis=1)
        grad_t = jnp.concatenate(grads_t, axis=1)
        att_o[:, g] = dot(low, vst).astype(BF16).reshape(shape)
        qg_o[:, g] = dot(grad, kst).astype(BF16).reshape(shape)
        kg_o[:, g] = dot(grad_t, stack(q)).astype(BF16).reshape(shape)
        vg_o[:, g] = dot(low_t, stack(og)).astype(BF16).reshape(shape)
        return carry

    lax.fori_loop(0, groups, one_group, 0)

    def back(t, carry):
        total = dot(qg_o[t].reshape(flat, chans), wqt[...])
        total = total + dot(kg_o[t].reshape(flat, chans), wkt[...])
        total = total + dot(vg_o[t].reshape(flat, chans), wvt[...])
        cols_o[t] = total.astype(BF16).reshape(groups, span, chans)
        return carry

    lax.fori_loop(0, sources, back, 0)


def weight_grads_kernel(hid, cot, att, qg, kg, vg, out_ref):
    sources, groups, span, chans = hid.shape
    flat = groups * span
    out_ref[...] = jnp.zeros(out_ref.shape, F32)

    def one(t, carry):
        ht = hid[t].reshape(flat, chans).T
        for i, ref in enumerate((qg, kg, vg)):
            out_ref[i] += dot(ht, ref[t].reshape(flat, chans))
        out_ref[3] += dot(att[t].reshape(flat, chans).T, cot[t].reshape(flat, chans))
        return carry

    lax.fori_loop(0, sources, one, 0)


def hidden_grad_kernel(back_ref, cot_ref, out_ref, first_ref, last_ref):
    frames, rows, cols, chans = cot_ref.shape
    real = rows * cols // PIXEL_BLOCK
    back = back_ref[0:real].astype(F32)
    for f in range(frames):
        piece = back[:, f * PIXEL_BLOCK : (f + 1) * PIXEL_BLOCK].reshape(rows, cols, chans)
        total = (cot_ref[f].astype(F32) + piece).astype(BF16)
        out_ref[f] = total
        first_ref[f] = total[0]
        last_ref[f] = total[rows - 1]


def conv_grad_kernel(top_ref, cells_ref, bottom_ref, grad_ref, out_ref, ext):
    frames, rows, cols, chans = cells_ref.shape
    out_ref[...] = jnp.zeros(out_ref.shape, F32)

    def one_frame(f, carry):
        ext[0] = top_ref[f]
        ext[1 : rows + 1] = cells_ref[f]
        ext[rows + 1] = bottom_ref[f]
        grad = grad_ref[f].reshape(rows * cols, chans)
        wide = grad.astype(F32)
        moved = [
            shifted(wide, 1, rows, cols).astype(BF16),
            grad,
            shifted(wide, -1, rows, cols).astype(BF16),
        ]
        for a in range(3):
            turned = ext[a : a + rows].reshape(rows * cols, chans).T
            for b in range(3):
                at = (3 * a + b) * chans
                out_ref[at : at + chans] += dot(turned, moved[b])
        return carry

    lax.fori_loop(0, frames, one_frame, 0)


def hops(sizes):
    space, tm = sizes
    first = [("space", 1)]
    rest = []
    stride = 2
    while stride < space:
        rest.append(("space", stride))
        stride *= 2
    stride = 1
    while stride < tm:
        rest.append(("tm", stride))
        stride *= 2
    return [first + rest[p:] + rest[:p] for p in range(3)], first + rest


def reduce_kernel(plan, greet, part_rows, x_ref, out_ref, acc, low, send_sems, recv_sems, *recvs):
    def bit_and_partner(axis, stride):
        me = lax.axis_index(axis)
        bit = (me // stride) % 2
        return bit, me + (1 - 2 * bit) * stride

    barrier = pltpu.get_barrier_semaphore()
    for axis, stride in greet:
        _, partner = bit_and_partner(axis, stride)
        pl.semaphore_signal(barrier, inc=1, device_id={axis: partner}, device_id_type=MESH)
    pl.semaphore_wait(barrier, len(greet))

    parts, steps = len(plan), len(plan[0])
    offs = [p * part_rows for p in range(parts)]
    size = part_rows
    for s in range(steps):
        half = size // 2
        src = x_ref if s == 0 else acc
        copies, keeps = [], []
        for p in range(parts):
            axis, stride = plan[p][s]
            bit, partner = bit_and_partner(axis, stride)
            send = pl.multiple_of(offs[p] + (1 - bit) * half, 16)
            keeps.append(pl.multiple_of(offs[p] + bit * half, 16))
            copy = pltpu.make_async_remote_copy(
                src_ref=src.at[pl.ds(send, half)],
                dst_ref=recvs[s].at[p],
                send_sem=send_sems.at[s, p],
                recv_sem=recv_sems.at[s, p],
                device_id={axis: partner},
                device_id_type=MESH,
            )
            copy.start()
            copies.append(copy)
        for p in range(parts):
            copies[p].wait()
            acc[pl.ds(keeps[p], half)] = src[pl.ds(keeps[p], half)] + recvs[s][p]
        offs, size = keeps, half
    for p in range(parts):
        low[pl.ds(offs[p], size)] = acc[pl.ds(offs[p], size)].astype(BF16)
    for s in range(steps - 1, -1, -1):
        copies, wider = [], []
        for p in range(parts):
            axis, stride = plan[p][s]
            bit, partner = bit_and_partner(axis, stride)
            mine = low.at[pl.ds(offs[p], size)]
            copy = pltpu.make_async_remote_copy(
                src_ref=mine,
                dst_ref=mine,
                send_sem=send_sems.at[steps + s, p],
                recv_sem=recv_sems.at[steps + s, p],
                device_id={axis: partner},
                device_id_type=MESH,
            )
            copy.start()
            copies.append(copy)
            wider.append(pl.multiple_of(offs[p] - bit * size, 16))
        for copy in copies:
            copy.wait()
        offs, size = wider, size * 2
    out_ref[...] = low[...].astype(F32)


def total_over_devices(arr, sizes, part_rows):
    plan, greet = hops(sizes)
    steps, parts = len(greet), len(plan)
    chans = arr.shape[1]
    scratch = [
        pltpu.VMEM(arr.shape, F32),
        pltpu.VMEM(arr.shape, BF16),
        pltpu.SemaphoreType.DMA((2 * steps, parts)),
        pltpu.SemaphoreType.DMA((2 * steps, parts)),
    ]
    scratch += [pltpu.VMEM((parts, part_rows >> (s + 1), chans), F32) for s in range(steps)]
    return call(
        functools.partial(reduce_kernel, plan, greet, part_rows),
        shape_of(arr.shape, F32),
        (arr,),
        scratch,
        collective_id=0,
        has_side_effects=True,
    )


def halo(first, last):
    count = lax.axis_size("space")
    up = [(i, i + 1) for i in range(count - 1)]
    down = [(i + 1, i) for i in range(count - 1)]
    return lax.ppermute(last, "space", up), lax.ppermute(first, "space", down)


def on_device(latents, cotangent, conv_weight, query_weight, key_weight, value_weight, out_weight):
    frames, rows, cols, chans = latents.shape
    sizes = (lax.axis_size("space"), lax.axis_size("tm"))
    space, tm = sizes
    whole_count = frames * tm * rows * space * cols
    norm = 1.0 / jnp.sqrt(jnp.float32(whole_count))
    per_source = -(-(rows * cols // PIXEL_BLOCK) // tm)
    groups = per_source * tm
    span = frames * PIXEL_BLOCK
    grouped = (tm, per_source, span, chans)

    def exchange(arr):
        return lax.all_to_all(arr, "tm", split_axis=0, concat_axis=0, tiled=True)

    top, bottom = halo(latents[:, 0], latents[:, rows - 1])
    cot_groups = call(regroup_kernel, shape_of((groups, span, chans), BF16), (cotangent,))
    cot_all = exchange(cot_groups).reshape(grouped)
    weights = conv_weight.reshape(9, chans, chans)
    hidden = convolve(top, latents, bottom, weights, groups)
    hid_all = exchange(hidden).reshape(grouped)
    tile = shape_of(grouped, BF16)
    attn_cols, attended, query_grad, key_grad, value_grad = call(
        attend_kernel,
        (tile,) * 5,
        (
            hid_all,
            cot_all,
            query_weight,
            key_weight,
            value_weight,
            out_weight.T,
            query_weight.T,
            key_weight.T,
            value_weight.T,
        ),
        [pltpu.VMEM(grouped, BF16)] * 4,
        flops=20 * hid_all.size * chans,
    )
    attn_back = exchange(attn_cols.reshape(groups, span, chans))
    small = call(
        weight_grads_kernel,
        shape_of((4, chans, chans), F32),
        (hid_all, cot_all, attended, query_grad, key_grad, value_grad),
        flops=8 * hid_all.size * chans,
    )
    small = lax.psum(small, ("space", "tm")) * norm
    hidden_grad, first, last = call(
        hidden_grad_kernel,
        (
            shape_of(latents.shape, BF16),
            shape_of((frames, cols, chans), BF16),
            shape_of((frames, cols, chans), BF16),
        ),
        (attn_back, cotangent),
    )
    grad_top, grad_bottom = halo(first, last)
    devices = space * tm
    part_rows = -(-9 * chans // (3 * devices * 16)) * devices * 16
    conv_part = call(
        conv_grad_kernel,
        shape_of((3 * part_rows, chans), F32),
        (top, latents, bottom, hidden_grad),
        [pltpu.VMEM((rows + 2, cols, chans), BF16)],
        flops=18 * latents.size * chans,
    )
    turned = jnp.swapaxes(conv_weight[::-1, ::-1], 2, 3).reshape(9, chans, chans)
    grad_input = convolve(grad_top, hidden_grad, grad_bottom, turned)
    conv_total = total_over_devices(conv_part, sizes, part_rows)
    grad_conv = conv_total[: 9 * chans].reshape(3, 3, chans, chans) * norm
    return grad_input, grad_conv, small[0], small[1], small[2], small[3]


def solution(mesh):
    in_specs = (P("tm", "space", None, None), P("tm", "space", None, None), P(), P(), P(), P(), P())
    out_specs = (P("tm", "space", None, None), P(), P(), P(), P(), P())
    return jax.shard_map(
        on_device, mesh=mesh, in_specs=in_specs, out_specs=out_specs, check_vma=False
    )
```

```python
import functools

import jax
import jax.numpy as jnp
from jax import lax
from jax.experimental import pallas as pl
from jax.experimental.pallas import tpu as pltpu
from jax.sharding import PartitionSpec as P

HEAD_DIM = 64
PIXEL_BLOCK = 8
LANES = 128
F32 = jnp.float32
BF16 = jnp.bfloat16
VMEM_BYTES = 50 * 1024 * 1024
MESH = pl.DeviceIdType.MESH


def call(body, out_shape, args, scratch=(), flops=0, **params):
    size = sum(a.size * a.dtype.itemsize for a in args)
    return pl.pallas_call(
        body,
        out_shape=out_shape,
        in_specs=[pl.BlockSpec(memory_space=pltpu.VMEM)] * len(args),
        out_specs=jax.tree.map(lambda _: pl.BlockSpec(memory_space=pltpu.VMEM), out_shape),
        scratch_shapes=list(scratch),
        compiler_params=pltpu.CompilerParams(vmem_limit_bytes=VMEM_BYTES, **params),
        cost_estimate=pl.CostEstimate(flops=flops, bytes_accessed=2 * size, transcendentals=0),
    )(*args)


def shape_of(shape, dtype):
    return jax.ShapeDtypeStruct(shape, dtype)


def dot(left, right, dims=((1,), (0,))):
    return lax.dot_general(left, right, (dims, ((), ())), preferred_element_type=F32)


def shifted(arr, step, rows, cols, pad):
    chans = arr.shape[-1]
    edge = 7 if step < 0 else cols + 8
    pad[:, edge : edge + 1] = jnp.zeros((rows, 1, chans), F32)
    pad[:, 8 : cols + 8] = arr.reshape(rows, cols, chans)
    return pad[:, 8 + step : 8 + step + cols].reshape(rows * cols, chans)


def conv_frame(f, top_ref, cells_ref, bottom_ref, weight_ref, ext, pad):
    frames, rows, cols, chans = cells_ref.shape
    ext[0] = top_ref[f]
    ext[1 : rows + 1] = cells_ref[f]
    ext[rows + 1] = bottom_ref[f]
    total = cells_ref[f].reshape(rows * cols, chans).astype(F32)
    for b in range(3):
        part = None
        for a in range(3):
            piece = ext[a : a + rows].reshape(rows * cols, chans)
            prod = dot(piece, weight_ref[3 * a + b])
            part = prod if part is None else part + prod
        total = total + (part if b == 1 else shifted(part, b - 1, rows, cols, pad))
    return total


def conv_scratch(rows, cols, chans):
    return [pltpu.VMEM((rows + 2, cols, chans), BF16), pltpu.VMEM((rows, cols + 16, chans), F32)]


def regroup(parts, groups):
    chans = parts[0].shape[-1]
    cat = jnp.concatenate([part.reshape(-1, PIXEL_BLOCK, chans) for part in parts], axis=1)
    return cat.astype(BF16)


def regroup_kernel(cells_ref, out_ref):
    frames, rows, cols, chans = cells_ref.shape
    real = rows * cols // PIXEL_BLOCK
    parts = [cells_ref[f].reshape(rows * cols, chans).astype(F32) for f in range(frames)]
    out_ref[0:real] = regroup(parts, real)
    if out_ref.shape[0] > real:
        out_ref[real:] = jnp.zeros((out_ref.shape[0] - real,) + out_ref.shape[1:], BF16)


def conv_kernel(top_ref, cells_ref, bottom_ref, weight_ref, out_ref, ext, pad, held):
    frames, rows, cols, chans = cells_ref.shape

    def one_frame(f, carry):
        held[f] = conv_frame(f, top_ref, cells_ref, bottom_ref, weight_ref, ext, pad)
        return carry

    lax.fori_loop(0, frames, one_frame, 0)
    real = rows * cols // PIXEL_BLOCK
    out_ref[0:real] = regroup([held[f] for f in range(frames)], real)
    if out_ref.shape[0] > real:
        out_ref[real:] = jnp.zeros((out_ref.shape[0] - real,) + out_ref.shape[1:], BF16)


def convolve(top, cells, bottom, weight, groups):
    frames, rows, cols, chans = cells.shape
    return call(
        conv_kernel,
        shape_of((groups, frames * PIXEL_BLOCK, chans), BF16),
        (top, cells, bottom, weight),
        conv_scratch(rows, cols, chans) + [pltpu.VMEM((frames, rows * cols, chans), F32)],
        flops=18 * cells.size * chans,
    )


def attend_kernel(
    hid, cot, wq, wk, wv, wot, wqt, wkt, wvt, cols_o, att_o, qg_o, kg_o, vg_o, q_s, k_s, v_s, g_s
):
    sources, groups, span, chans = hid.shape
    heads = chans // HEAD_DIM
    scale = HEAD_DIM ** (-0.5)
    size = sources * span
    flat = groups * span

    def project(t, carry):
        h = hid[t].reshape(flat, chans)
        for ref, w in ((q_s, wq), (k_s, wk), (v_s, wv)):
            ref[t] = dot(h, w[...]).astype(BF16).reshape(groups, span, chans)
        c = cot[t].reshape(flat, chans)
        g_s[t] = dot(c, wot[...]).astype(BF16).reshape(groups, span, chans)
        return carry

    lax.fori_loop(0, sources, project, 0)

    place = lax.broadcasted_iota(jnp.int32, (1, chans), 1)
    head_masks = [
        jnp.where((place >= h * HEAD_DIM) & (place < (h + 1) * HEAD_DIM), 1.0, 0.0).astype(BF16)
        for h in range(heads)
    ]
    left = lax.broadcasted_iota(jnp.int32, (size, size), 0)
    right = lax.broadcasted_iota(jnp.int32, (size, size), 1)
    same = (left & (PIXEL_BLOCK - 1)) == (right & (PIXEL_BLOCK - 1))

    def one_group(g, carry):
        def get(ref):
            return ref[:, g].reshape(size, chans)

        def stack(arr):
            return jnp.concatenate([arr * m for m in head_masks], axis=0)

        q, k, v, og = get(q_s), get(k_s), get(v_s), get(g_s)
        kst, vst = stack(k), stack(v)
        scores = dot(q, kst, ((1,), (1,))) * scale
        dprobs = dot(og, vst, ((1,), (1,)))
        lows, lows_t, grads, grads_t = [], [], [], []
        for h in range(heads):
            block = slice(h * size, (h + 1) * size)
            s = jnp.where(same, scores[:, block], -1e30)
            e = jnp.exp(s - jnp.max(s, axis=1, keepdims=True))
            prob = e / jnp.sum(e, axis=1, keepdims=True)
            dp = dprobs[:, block]
            ds = prob * (dp - jnp.sum(prob * dp, axis=1, keepdims=True)) * scale
            low, grad = prob.astype(BF16), ds.astype(BF16)
            lows.append(low)
            grads.append(grad)
            lows_t.append(low.T)
            grads_t.append(grad.T)
        shape = (sources, span, chans)
        low = jnp.concatenate(lows, axis=1)
        grad = jnp.concatenate(grads, axis=1)
        low_t = jnp.concatenate(lows_t, axis=1)
        grad_t = jnp.concatenate(grads_t, axis=1)
        att_o[:, g] = dot(low, vst).astype(BF16).reshape(shape)
        qg_o[:, g] = dot(grad, kst).astype(BF16).reshape(shape)
        kg_o[:, g] = dot(grad_t, stack(q)).astype(BF16).reshape(shape)
        vg_o[:, g] = dot(low_t, stack(og)).astype(BF16).reshape(shape)
        return carry

    lax.fori_loop(0, groups, one_group, 0)

    def back(t, carry):
        total = dot(qg_o[t].reshape(flat, chans), wqt[...])
        total = total + dot(kg_o[t].reshape(flat, chans), wkt[...])
        total = total + dot(vg_o[t].reshape(flat, chans), wvt[...])
        cols_o[t] = total.astype(BF16).reshape(groups, span, chans)
        return carry

    lax.fori_loop(0, sources, back, 0)


def pack_places(count, chans):
    whole, rest = chans // LANES, chans % LANES
    places, row = [], 0
    for m in range(count):
        for block in range(whole):
            places.append((row, 0, m, block * LANES, LANES))
            row += chans
    lane = 0
    for m in range(count if rest else 0):
        places.append((row, lane, m, whole * LANES, rest))
        lane += rest
        if lane + rest > LANES:
            row, lane = row + chans, 0
    return places, row + (chans if lane else 0)


def pack(total, out_ref):
    count, chans, _ = total.shape
    places, used = pack_places(count, chans)
    out_ref[used:] = jnp.zeros((out_ref.shape[0] - used, LANES), F32)
    if places[-1][1] + places[-1][4] < LANES:
        out_ref[used - chans : used] = jnp.zeros((chans, LANES), F32)
    for row, lane, m, col, width in places:
        out_ref[row : row + chans, lane : lane + width] = total[m, :, col : col + width]


def part_size(count, chans, parts, devices):
    unit = parts * devices * 16
    return -(-pack_places(count, chans)[1] // unit) * devices * 16


def weight_grads_kernel(hid, cot, att, qg, kg, vg, out_ref, total):
    sources, groups, span, chans = hid.shape
    flat = groups * span
    total[...] = jnp.zeros(total.shape, F32)

    def one(t, carry):
        ht = hid[t].reshape(flat, chans).T
        for i, ref in enumerate((qg, kg, vg)):
            total[i] += dot(ht, ref[t].reshape(flat, chans))
        total[3] += dot(att[t].reshape(flat, chans).T, cot[t].reshape(flat, chans))
        return carry

    lax.fori_loop(0, sources, one, 0)
    pack(total, out_ref)


def hidden_grad_kernel(back_ref, cot_ref, out_ref, first_ref, last_ref):
    frames, rows, cols, chans = cot_ref.shape
    real = rows * cols // PIXEL_BLOCK
    back = back_ref[0:real].astype(F32)
    for f in range(frames):
        piece = back[:, f * PIXEL_BLOCK : (f + 1) * PIXEL_BLOCK].reshape(rows, cols, chans)
        total = (cot_ref[f].astype(F32) + piece).astype(BF16)
        out_ref[f] = total
        first_ref[f] = total[0]
        last_ref[f] = total[rows - 1]


def conv_grad_kernel(top_ref, cells_ref, bottom_ref, grad_ref, out_ref, ext, pad, total):
    frames, rows, cols, chans = cells_ref.shape
    total[...] = jnp.zeros(total.shape, F32)

    def one_frame(f, carry):
        ext[0] = top_ref[f]
        ext[1 : rows + 1] = cells_ref[f]
        ext[rows + 1] = bottom_ref[f]
        grad = grad_ref[f].reshape(rows * cols, chans)
        wide = grad.astype(F32)
        moved = [
            shifted(wide, 1, rows, cols, pad).astype(BF16),
            grad,
            shifted(wide, -1, rows, cols, pad).astype(BF16),
        ]
        for a in range(3):
            turned = ext[a : a + rows].reshape(rows * cols, chans).T
            for b in range(3):
                total[3 * a + b] += dot(turned, moved[b])
        return carry

    lax.fori_loop(0, frames, one_frame, 0)
    pack(total, out_ref)


def hops(sizes, parts, links_first):
    space, tm = sizes
    first, planes, line = [("space", 1)], [], []
    stride = 2
    while stride < space:
        planes.append(("space", stride))
        stride *= 2
    stride = 1
    while stride < tm:
        line.append(("tm", stride))
        stride *= 2
    if links_first:
        plan = [first + planes[p:] + planes[:p] + line for p in range(parts)]
    else:
        rest = planes + line
        plan = [first + rest[p:] + rest[:p] for p in range(parts)]
    return plan, first + planes + line


def reduce_kernel(plan, greet, part_rows, norm, beside, *refs):
    if beside:
        x_ref, top_ref, cells_ref, bottom_ref, weight_ref, out_ref, result_ref = refs[:7]
        ext, pad, acc, low, send_sems, recv_sems, *recvs = refs[7:]
    else:
        x_ref, out_ref, acc, low, send_sems, recv_sems, *recvs = refs

    def bit_and_partner(axis, stride):
        me = lax.axis_index(axis)
        bit = (me // stride) % 2
        return bit, me + (1 - 2 * bit) * stride

    barrier = pltpu.get_barrier_semaphore()
    for axis, stride in greet:
        _, partner = bit_and_partner(axis, stride)
        pl.semaphore_signal(barrier, inc=1, device_id={axis: partner}, device_id_type=MESH)
    pl.semaphore_wait(barrier, len(greet))

    parts, steps = len(plan), len(plan[0])
    offs = [p * part_rows for p in range(parts)]
    size = part_rows
    for s in range(steps):
        half = size // 2
        src = x_ref if s == 0 else acc
        copies, keeps = [], []
        for p in range(parts):
            axis, stride = plan[p][s]
            bit, partner = bit_and_partner(axis, stride)
            send = pl.multiple_of(offs[p] + (1 - bit) * half, 16)
            keeps.append(pl.multiple_of(offs[p] + bit * half, 16))
            copy = pltpu.make_async_remote_copy(
                src_ref=src.at[pl.ds(send, half)],
                dst_ref=recvs[s].at[p],
                send_sem=send_sems.at[s, p],
                recv_sem=recv_sems.at[s, p],
                device_id={axis: partner},
                device_id_type=MESH,
            )
            copy.start()
            copies.append(copy)
        if beside:
            frames, rows, cols, chans = cells_ref.shape
            for f in range(s, frames, steps):
                total = conv_frame(f, top_ref, cells_ref, bottom_ref, weight_ref, ext, pad)
                result_ref[f] = total.astype(BF16).reshape(rows, cols, chans)
        for p in range(parts):
            copies[p].wait()
            acc[pl.ds(keeps[p], half)] = src[pl.ds(keeps[p], half)] + recvs[s][p]
        offs, size = keeps, half
    for p in range(parts):
        low[pl.ds(offs[p], size)] = acc[pl.ds(offs[p], size)].astype(BF16)
    for s in range(steps - 1, -1, -1):
        copies, wider = [], []
        for p in range(parts):
            axis, stride = plan[p][s]
            bit, partner = bit_and_partner(axis, stride)
            mine = low.at[pl.ds(offs[p], size)]
            copy = pltpu.make_async_remote_copy(
                src_ref=mine,
                dst_ref=mine,
                send_sem=send_sems.at[steps + s, p],
                recv_sem=recv_sems.at[steps + s, p],
                device_id={axis: partner},
                device_id_type=MESH,
            )
            copy.start()
            copies.append(copy)
            wider.append(pl.multiple_of(offs[p] - bit * size, 16))
        for copy in copies:
            copy.wait()
        offs, size = wider, size * 2
    count, chans, _ = out_ref.shape
    for row, lane, m, col, width in pack_places(count, chans)[0]:
        piece = low[row : row + chans, lane : lane + width].astype(F32)
        out_ref[m, :, col : col + width] = piece * norm


def total_over_devices(arr, count, chans, norm, sizes, parts, part_rows, links_first, number, conv=()):
    plan, greet = hops(sizes, parts, links_first)
    steps = len(greet)
    out = shape_of((count, chans, chans), F32)
    scratch = []
    if conv:
        out = (out, shape_of(conv[1].shape, BF16))
        scratch += conv_scratch(*conv[1].shape[1:])
    scratch += [
        pltpu.VMEM(arr.shape, F32),
        pltpu.VMEM(arr.shape, BF16),
        pltpu.SemaphoreType.DMA((2 * steps, parts)),
        pltpu.SemaphoreType.DMA((2 * steps, parts)),
    ]
    scratch += [pltpu.VMEM((parts, part_rows >> (s + 1), LANES), F32) for s in range(steps)]
    return call(
        functools.partial(reduce_kernel, plan, greet, part_rows, norm, bool(conv)),
        out,
        (arr,) + conv,
        scratch,
        collective_id=number,
        has_side_effects=True,
    )


def halo(first, last):
    count = lax.axis_size("space")
    up = [(i, i + 1) for i in range(count - 1)]
    down = [(i + 1, i) for i in range(count - 1)]
    return lax.ppermute(last, "space", up), lax.ppermute(first, "space", down)


def on_device(latents, cotangent, conv_weight, query_weight, key_weight, value_weight, out_weight):
    frames, rows, cols, chans = latents.shape
    sizes = (lax.axis_size("space"), lax.axis_size("tm"))
    space, tm = sizes
    whole_count = frames * tm * rows * space * cols
    norm = float(whole_count) ** -0.5
    devices = space * tm
    per_source = -(-(rows * cols // PIXEL_BLOCK) // tm)
    groups = per_source * tm
    span = frames * PIXEL_BLOCK
    grouped = (tm, per_source, span, chans)

    def exchange(arr):
        return lax.all_to_all(arr, "tm", split_axis=0, concat_axis=0, tiled=True)

    top, bottom = halo(latents[:, 0], latents[:, rows - 1])
    cot_groups = call(regroup_kernel, shape_of((groups, span, chans), BF16), (cotangent,))
    cot_all = exchange(cot_groups).reshape(grouped)
    weights = conv_weight.reshape(9, chans, chans)
    hidden = convolve(top, latents, bottom, weights, groups)
    hid_all = exchange(hidden).reshape(grouped)
    tile = shape_of(grouped, BF16)
    attn_cols, attended, query_grad, key_grad, value_grad = call(
        attend_kernel,
        (tile,) * 5,
        (
            hid_all,
            cot_all,
            query_weight,
            key_weight,
            value_weight,
            out_weight.T,
            query_weight.T,
            key_weight.T,
            value_weight.T,
        ),
        [pltpu.VMEM(grouped, BF16)] * 4,
        flops=20 * hid_all.size * chans,
    )
    attn_back = exchange(attn_cols.reshape(groups, span, chans))
    small_rows = part_size(4, chans, 2, devices)
    small = call(
        weight_grads_kernel,
        shape_of((2 * small_rows, LANES), F32),
        (hid_all, cot_all, attended, query_grad, key_grad, value_grad),
        [pltpu.VMEM((4, chans, chans), F32)],
        flops=8 * hid_all.size * chans,
    )
    small = total_over_devices(small, 4, chans, norm, sizes, 2, small_rows, True, 0)
    attn_back, small = lax.optimization_barrier((attn_back, small))
    hidden_grad, first, last = call(
        hidden_grad_kernel,
        (
            shape_of(latents.shape, BF16),
            shape_of((frames, cols, chans), BF16),
            shape_of((frames, cols, chans), BF16),
        ),
        (attn_back, cotangent),
    )
    grad_top, grad_bottom = halo(first, last)
    part_rows = part_size(9, chans, 3, devices)
    conv_part = call(
        conv_grad_kernel,
        shape_of((3 * part_rows, LANES), F32),
        (top, latents, bottom, hidden_grad),
        conv_scratch(rows, cols, chans) + [pltpu.VMEM((9, chans, chans), F32)],
        flops=18 * latents.size * chans,
    )
    turned = jnp.swapaxes(conv_weight[::-1, ::-1], 2, 3).reshape(9, chans, chans)
    grad_conv, grad_input = total_over_devices(
        conv_part,
        9,
        chans,
        norm,
        sizes,
        3,
        part_rows,
        False,
        1,
        (grad_top, hidden_grad, grad_bottom, turned),
    )
    grad_conv = grad_conv.reshape(3, 3, chans, chans)
    return grad_input, grad_conv, small[0], small[1], small[2], small[3]


def solution(mesh):
    in_specs = (P("tm", "space", None, None), P("tm", "space", None, None), P(), P(), P(), P(), P())
    out_specs = (P("tm", "space", None, None), P(), P(), P(), P(), P())
    return jax.shard_map(
        on_device, mesh=mesh, in_specs=in_specs, out_specs=out_specs, check_vma=False
    )
```

```python
import functools

import jax
import jax.numpy as jnp
from jax import lax
from jax.experimental import pallas as pl
from jax.experimental.pallas import tpu as pltpu
from jax.sharding import PartitionSpec as P

HEAD_DIM = 64
PIXEL_BLOCK = 8
LANES = 128
F32 = jnp.float32
BF16 = jnp.bfloat16
VMEM_BYTES = 50 * 1024 * 1024
MESH = pl.DeviceIdType.MESH


def call(body, out_shape, args, scratch=(), flops=0, **params):
    size = sum(a.size * a.dtype.itemsize for a in args)
    return pl.pallas_call(
        body,
        out_shape=out_shape,
        in_specs=[pl.BlockSpec(memory_space=pltpu.VMEM)] * len(args),
        out_specs=jax.tree.map(lambda _: pl.BlockSpec(memory_space=pltpu.VMEM), out_shape),
        scratch_shapes=list(scratch),
        compiler_params=pltpu.CompilerParams(vmem_limit_bytes=VMEM_BYTES, **params),
        cost_estimate=pl.CostEstimate(flops=flops, bytes_accessed=2 * size, transcendentals=0),
    )(*args)


def shape_of(shape, dtype):
    return jax.ShapeDtypeStruct(shape, dtype)


def dot(left, right, dims=((1,), (0,))):
    return lax.dot_general(left, right, (dims, ((), ())), preferred_element_type=F32)


def shifted(arr, step, rows, cols, pad):
    chans = arr.shape[-1]
    edge = 7 if step < 0 else cols + 8
    pad[:, edge : edge + 1] = jnp.zeros((rows, 1, chans), F32)
    pad[:, 8 : cols + 8] = arr.reshape(rows, cols, chans)
    return pad[:, 8 + step : 8 + step + cols].reshape(rows * cols, chans)


def conv_frame(f, top_ref, cells_ref, bottom_ref, weight_ref, ext, pad):
    frames, rows, cols, chans = cells_ref.shape
    ext[0] = top_ref[f]
    ext[1 : rows + 1] = cells_ref[f]
    ext[rows + 1] = bottom_ref[f]
    total = cells_ref[f].reshape(rows * cols, chans).astype(F32)
    for b in range(3):
        part = None
        for a in range(3):
            piece = ext[a : a + rows].reshape(rows * cols, chans)
            prod = dot(piece, weight_ref[3 * a + b])
            part = prod if part is None else part + prod
        total = total + (part if b == 1 else shifted(part, b - 1, rows, cols, pad))
    return total


def conv_scratch(rows, cols, chans):
    return [pltpu.VMEM((rows + 2, cols, chans), BF16), pltpu.VMEM((rows, cols + 16, chans), F32)]


def regroup(parts, groups):
    chans = parts[0].shape[-1]
    cat = jnp.concatenate([part.reshape(-1, PIXEL_BLOCK, chans) for part in parts], axis=1)
    return cat.astype(BF16)


def fill(out_ref, cells, start):
    count = min(out_ref.shape[0], cells.shape[0] - start)
    if count > 0:
        out_ref[0:count] = cells[start : start + count]
    if out_ref.shape[0] > count:
        out_ref[count:] = jnp.zeros((out_ref.shape[0] - count,) + out_ref.shape[1:], BF16)


def regroup_kernel(halves, cells_ref, out_ref):
    frames, rows, cols, chans = cells_ref.shape
    real = rows * cols // PIXEL_BLOCK
    parts = [cells_ref[f].reshape(rows * cols, chans).astype(F32) for f in range(frames)]
    cells = regroup(parts, real)
    per = sum(halves)
    owners = out_ref.shape[0] // per
    first = halves[0] * owners
    for owner in range(owners):
        at = owner * per
        for start, length, base in (
            (owner * halves[0], halves[0], 0),
            (first + owner * halves[1], halves[1], halves[0]),
        ):
            fill(out_ref.at[at + base : at + base + length], cells, min(start, real))


def conv_kernel(top_ref, cells_ref, bottom_ref, weight_ref, one_ref, two_ref, ext, pad, held):
    frames, rows, cols, chans = cells_ref.shape

    def one_frame(f, carry):
        held[f] = conv_frame(f, top_ref, cells_ref, bottom_ref, weight_ref, ext, pad)
        return carry

    lax.fori_loop(0, frames, one_frame, 0)
    real = rows * cols // PIXEL_BLOCK
    cells = regroup([held[f] for f in range(frames)], real)
    fill(one_ref, cells, 0)
    fill(two_ref, cells, one_ref.shape[0])


def convolve(top, cells, bottom, weight, counts):
    frames, rows, cols, chans = cells.shape
    return call(
        conv_kernel,
        tuple(shape_of((count, frames * PIXEL_BLOCK, chans), BF16) for count in counts),
        (top, cells, bottom, weight),
        conv_scratch(rows, cols, chans) + [pltpu.VMEM((frames, rows * cols, chans), F32)],
        flops=18 * cells.size * chans,
    )


def attend_kernel(
    base, hid, cot, wq, wk, wv, wot, wqt, wkt, wvt, cols_o, att_o, qg_o, kg_o, vg_o, q_s, k_s, v_s, g_s
):
    sources, groups, span, chans = hid.shape
    heads = chans // HEAD_DIM
    scale = HEAD_DIM ** (-0.5)
    size = sources * span
    flat = groups * span

    def project(t, carry):
        h = hid[t].reshape(flat, chans)
        for ref, w in ((q_s, wq), (k_s, wk), (v_s, wv)):
            ref[t] = dot(h, w[...]).astype(BF16).reshape(groups, span, chans)
        c = cot[t, base : base + groups].reshape(flat, chans)
        g_s[t] = dot(c, wot[...]).astype(BF16).reshape(groups, span, chans)
        return carry

    lax.fori_loop(0, sources, project, 0)

    place = lax.broadcasted_iota(jnp.int32, (1, chans), 1)
    head_masks = [
        jnp.where((place >= h * HEAD_DIM) & (place < (h + 1) * HEAD_DIM), 1.0, 0.0).astype(BF16)
        for h in range(heads)
    ]
    left = lax.broadcasted_iota(jnp.int32, (size, size), 0)
    right = lax.broadcasted_iota(jnp.int32, (size, size), 1)
    same = (left & (PIXEL_BLOCK - 1)) == (right & (PIXEL_BLOCK - 1))

    def one_group(g, carry):
        def get(ref):
            return ref[:, g].reshape(size, chans)

        def stack(arr):
            return jnp.concatenate([arr * m for m in head_masks], axis=0)

        q, k, v, og = get(q_s), get(k_s), get(v_s), get(g_s)
        kst, vst = stack(k), stack(v)
        scores = dot(q, kst, ((1,), (1,))) * scale
        dprobs = dot(og, vst, ((1,), (1,)))
        lows, lows_t, grads, grads_t = [], [], [], []
        for h in range(heads):
            block = slice(h * size, (h + 1) * size)
            s = jnp.where(same, scores[:, block], -1e30)
            e = jnp.exp(s - jnp.max(s, axis=1, keepdims=True))
            prob = e / jnp.sum(e, axis=1, keepdims=True)
            dp = dprobs[:, block]
            ds = prob * (dp - jnp.sum(prob * dp, axis=1, keepdims=True)) * scale
            low, grad = prob.astype(BF16), ds.astype(BF16)
            lows.append(low)
            grads.append(grad)
            lows_t.append(low.T)
            grads_t.append(grad.T)
        shape = (sources, span, chans)
        low = jnp.concatenate(lows, axis=1)
        grad = jnp.concatenate(grads, axis=1)
        low_t = jnp.concatenate(lows_t, axis=1)
        grad_t = jnp.concatenate(grads_t, axis=1)
        att_o[:, g] = dot(low, vst).astype(BF16).reshape(shape)
        qg_o[:, g] = dot(grad, kst).astype(BF16).reshape(shape)
        kg_o[:, g] = dot(grad_t, stack(q)).astype(BF16).reshape(shape)
        vg_o[:, g] = dot(low_t, stack(og)).astype(BF16).reshape(shape)
        return carry

    lax.fori_loop(0, groups, one_group, 0)

    def back(t, carry):
        total = dot(qg_o[t].reshape(flat, chans), wqt[...])
        total = total + dot(kg_o[t].reshape(flat, chans), wkt[...])
        total = total + dot(vg_o[t].reshape(flat, chans), wvt[...])
        cols_o[t] = total.astype(BF16).reshape(groups, span, chans)
        return carry

    lax.fori_loop(0, sources, back, 0)


def pack_places(count, chans):
    whole, rest = chans // LANES, chans % LANES
    places, row = [], 0
    for m in range(count):
        for block in range(whole):
            places.append((row, 0, m, block * LANES, LANES))
            row += chans
    lane = 0
    for m in range(count if rest else 0):
        places.append((row, lane, m, whole * LANES, rest))
        lane += rest
        if lane + rest > LANES:
            row, lane = row + chans, 0
    return places, row + (chans if lane else 0)


def pack(total, out_ref):
    count, chans, _ = total.shape
    places, used = pack_places(count, chans)
    out_ref[used:] = jnp.zeros((out_ref.shape[0] - used, LANES), F32)
    if places[-1][1] + places[-1][4] < LANES:
        out_ref[used - chans : used] = jnp.zeros((chans, LANES), F32)
    for row, lane, m, col, width in places:
        out_ref[row : row + chans, lane : lane + width] = total[m, :, col : col + width]


def part_size(count, chans, parts, devices):
    unit = parts * devices * 16
    return -(-pack_places(count, chans)[1] // unit) * devices * 16


def weight_grads_kernel(cot, *refs):
    halves, (out_ref, total) = (refs[0:5], refs[5:10]), refs[10:]
    total[...] = jnp.zeros(total.shape, F32)

    def one(t, carry):
        base = 0
        for hid, att, qg, kg, vg in halves:
            _, groups, span, chans = hid.shape
            flat = groups * span
            ht = hid[t].reshape(flat, chans).T
            for i, ref in enumerate((qg, kg, vg)):
                total[i] += dot(ht, ref[t].reshape(flat, chans))
            c = cot[t, base : base + groups].reshape(flat, chans)
            total[3] += dot(att[t].reshape(flat, chans).T, c)
            base += groups
        return carry

    lax.fori_loop(0, cot.shape[0], one, 0)
    pack(total, out_ref)


def hidden_grad_kernel(one_ref, two_ref, cot_ref, out_ref, first_ref, last_ref):
    frames, rows, cols, chans = cot_ref.shape
    real = rows * cols // PIXEL_BLOCK
    rest = real - one_ref.shape[0]
    back = jnp.concatenate([one_ref[...].astype(F32), two_ref[0:rest].astype(F32)], axis=0)
    for f in range(frames):
        piece = back[:, f * PIXEL_BLOCK : (f + 1) * PIXEL_BLOCK].reshape(rows, cols, chans)
        total = (cot_ref[f].astype(F32) + piece).astype(BF16)
        out_ref[f] = total
        first_ref[f] = total[0]
        last_ref[f] = total[rows - 1]


def conv_grad_kernel(top_ref, cells_ref, bottom_ref, grad_ref, out_ref, ext, pad, total):
    frames, rows, cols, chans = cells_ref.shape
    total[...] = jnp.zeros(total.shape, F32)

    def one_frame(f, carry):
        ext[0] = top_ref[f]
        ext[1 : rows + 1] = cells_ref[f]
        ext[rows + 1] = bottom_ref[f]
        grad = grad_ref[f].reshape(rows * cols, chans)
        wide = grad.astype(F32)
        moved = [
            shifted(wide, 1, rows, cols, pad).astype(BF16),
            grad,
            shifted(wide, -1, rows, cols, pad).astype(BF16),
        ]
        for a in range(3):
            turned = ext[a : a + rows].reshape(rows * cols, chans).T
            for b in range(3):
                total[3 * a + b] += dot(turned, moved[b])
        return carry

    lax.fori_loop(0, frames, one_frame, 0)
    pack(total, out_ref)


def hops(sizes, parts, links_first):
    space, tm = sizes
    first, planes, line = [("space", 1)], [], []
    stride = 2
    while stride < space:
        planes.append(("space", stride))
        stride *= 2
    stride = 1
    while stride < tm:
        line.append(("tm", stride))
        stride *= 2
    if links_first:
        plan = [first + planes[p:] + planes[:p] + line for p in range(parts)]
    else:
        rest = planes + line
        plan = [first + rest[p:] + rest[:p] for p in range(parts)]
    return plan, first + planes + line


def reduce_kernel(plan, greet, part_rows, beside, *refs):
    if beside:
        x_ref, top_ref, cells_ref, bottom_ref, weight_ref, out_ref, result_ref = refs[:7]
        ext, pad, acc, low, send_sems, recv_sems, *recvs = refs[7:]
    else:
        x_ref, out_ref, acc, low, send_sems, recv_sems, *recvs = refs

    def bit_and_partner(axis, stride):
        me = lax.axis_index(axis)
        bit = (me // stride) % 2
        return bit, me + (1 - 2 * bit) * stride

    barrier = pltpu.get_barrier_semaphore()
    for axis, stride in greet:
        _, partner = bit_and_partner(axis, stride)
        pl.semaphore_signal(barrier, inc=1, device_id={axis: partner}, device_id_type=MESH)
    pl.semaphore_wait(barrier, len(greet))

    parts, steps = len(plan), len(plan[0])
    offs = [p * part_rows for p in range(parts)]
    size = part_rows
    for s in range(steps):
        half = size // 2
        src = x_ref if s == 0 else acc
        copies, keeps = [], []
        for p in range(parts):
            axis, stride = plan[p][s]
            bit, partner = bit_and_partner(axis, stride)
            send = pl.multiple_of(offs[p] + (1 - bit) * half, 16)
            keeps.append(pl.multiple_of(offs[p] + bit * half, 16))
            copy = pltpu.make_async_remote_copy(
                src_ref=src.at[pl.ds(send, half)],
                dst_ref=recvs[s].at[p],
                send_sem=send_sems.at[s, p],
                recv_sem=recv_sems.at[s, p],
                device_id={axis: partner},
                device_id_type=MESH,
            )
            copy.start()
            copies.append(copy)
        if beside:
            frames, rows, cols, chans = cells_ref.shape
            for f in range(s, frames, steps):
                total = conv_frame(f, top_ref, cells_ref, bottom_ref, weight_ref, ext, pad)
                result_ref[f] = total.astype(BF16).reshape(rows, cols, chans)
        for p in range(parts):
            copies[p].wait()
            acc[pl.ds(keeps[p], half)] = src[pl.ds(keeps[p], half)] + recvs[s][p]
        offs, size = keeps, half
    for p in range(parts):
        low[pl.ds(offs[p], size)] = acc[pl.ds(offs[p], size)].astype(BF16)
    for s in range(steps - 1, -1, -1):
        copies, wider = [], []
        for p in range(parts):
            axis, stride = plan[p][s]
            bit, partner = bit_and_partner(axis, stride)
            mine = low.at[pl.ds(offs[p], size)]
            copy = pltpu.make_async_remote_copy(
                src_ref=mine,
                dst_ref=mine,
                send_sem=send_sems.at[steps + s, p],
                recv_sem=recv_sems.at[steps + s, p],
                device_id={axis: partner},
                device_id_type=MESH,
            )
            copy.start()
            copies.append(copy)
            wider.append(pl.multiple_of(offs[p] - bit * size, 16))
        for copy in copies:
            copy.wait()
        offs, size = wider, size * 2
    out_ref[...] = low[...]


def unpack_kernel(norm, packed_ref, out_ref):
    count, chans, _ = out_ref.shape
    for row, lane, m, col, width in pack_places(count, chans)[0]:
        piece = packed_ref[row : row + chans, lane : lane + width].astype(F32)
        out_ref[m, :, col : col + width] = piece * norm


def total_over_devices(arr, count, chans, norm, sizes, parts, part_rows, links_first, number, conv=()):
    plan, greet = hops(sizes, parts, links_first)
    steps = len(greet)
    out = shape_of(arr.shape, BF16)
    scratch = []
    if conv:
        out = (out, shape_of(conv[1].shape, BF16))
        scratch += conv_scratch(*conv[1].shape[1:])
    scratch += [
        pltpu.VMEM(arr.shape, F32),
        pltpu.VMEM(arr.shape, BF16),
        pltpu.SemaphoreType.DMA((2 * steps, parts)),
        pltpu.SemaphoreType.DMA((2 * steps, parts)),
    ]
    scratch += [pltpu.VMEM((parts, part_rows >> (s + 1), LANES), F32) for s in range(steps)]
    result = call(
        functools.partial(reduce_kernel, plan, greet, part_rows, bool(conv)),
        out,
        (arr,) + conv,
        scratch,
        collective_id=number,
        has_side_effects=True,
    )
    packed = result[0] if conv else result
    grads = call(
        functools.partial(unpack_kernel, norm), shape_of((count, chans, chans), F32), (packed,)
    )
    return (grads, result[1]) if conv else grads


def halo(first, last):
    count = lax.axis_size("space")
    up = [(i, i + 1) for i in range(count - 1)]
    down = [(i + 1, i) for i in range(count - 1)]
    return lax.ppermute(last, "space", up), lax.ppermute(first, "space", down)


def on_device(latents, cotangent, conv_weight, query_weight, key_weight, value_weight, out_weight):
    frames, rows, cols, chans = latents.shape
    sizes = (lax.axis_size("space"), lax.axis_size("tm"))
    space, tm = sizes
    whole_count = frames * tm * rows * space * cols
    norm = float(whole_count) ** -0.5
    devices = space * tm
    per_source = -(-(rows * cols // PIXEL_BLOCK) // tm)
    groups = per_source * tm
    span = frames * PIXEL_BLOCK
    halves = (-(-per_source // 2), per_source // 2)

    def exchange(arr):
        return lax.all_to_all(arr, "tm", split_axis=0, concat_axis=0, tiled=True)

    def owned(arr, count):
        return exchange(arr).reshape(tm, count, span, chans)

    top, bottom = halo(latents[:, 0], latents[:, rows - 1])
    cot_groups = call(
        functools.partial(regroup_kernel, halves),
        shape_of((groups, span, chans), BF16),
        (cotangent,),
    )
    cot_all = owned(cot_groups, per_source)
    weights = conv_weight.reshape(9, chans, chans)
    hidden = convolve(top, latents, bottom, weights, [tm * half for half in halves])
    backs, saved = [], []
    for i, half in enumerate(halves):
        hid = owned(hidden[i], half)
        tile = shape_of(hid.shape, BF16)
        attn_cols, *grads = call(
            functools.partial(attend_kernel, i * halves[0]),
            (tile,) * 5,
            (
                hid,
                cot_all,
                query_weight,
                key_weight,
                value_weight,
                out_weight.T,
                query_weight.T,
                key_weight.T,
                value_weight.T,
            ),
            [pltpu.VMEM(hid.shape, BF16)] * 4,
            flops=20 * hid.size * chans,
        )
        backs.append(exchange(attn_cols.reshape(tm * half, span, chans)))
        saved += [hid] + grads
    small_rows = part_size(4, chans, 2, devices)
    small = call(
        weight_grads_kernel,
        shape_of((2 * small_rows, LANES), F32),
        (cot_all, *saved),
        [pltpu.VMEM((4, chans, chans), F32)],
        flops=8 * cot_all.size * chans,
    )
    small = total_over_devices(small, 4, chans, norm, sizes, 2, small_rows, True, 0)
    backs, small = lax.optimization_barrier((backs, small))
    hidden_grad, first, last = call(
        hidden_grad_kernel,
        (
            shape_of(latents.shape, BF16),
            shape_of((frames, cols, chans), BF16),
            shape_of((frames, cols, chans), BF16),
        ),
        (*backs, cotangent),
    )
    grad_top, grad_bottom = halo(first, last)
    part_rows = part_size(9, chans, 3, devices)
    conv_part = call(
        conv_grad_kernel,
        shape_of((3 * part_rows, LANES), F32),
        (top, latents, bottom, hidden_grad),
        conv_scratch(rows, cols, chans) + [pltpu.VMEM((9, chans, chans), F32)],
        flops=18 * latents.size * chans,
    )
    turned = jnp.swapaxes(conv_weight[::-1, ::-1], 2, 3).reshape(9, chans, chans)
    grad_conv, grad_input = total_over_devices(
        conv_part,
        9,
        chans,
        norm,
        sizes,
        3,
        part_rows,
        False,
        1,
        (grad_top, hidden_grad, grad_bottom, turned),
    )
    grad_conv = grad_conv.reshape(3, 3, chans, chans)
    return grad_input, grad_conv, small[0], small[1], small[2], small[3]


def solution(mesh):
    in_specs = (P("tm", "space", None, None), P("tm", "space", None, None), P(), P(), P(), P(), P())
    out_specs = (P("tm", "space", None, None), P(), P(), P(), P(), P())
    return jax.shard_map(
        on_device, mesh=mesh, in_specs=in_specs, out_specs=out_specs, check_vma=False
    )
```

```python
import functools

import jax
import jax.numpy as jnp
from jax import lax
from jax.experimental import pallas as pl
from jax.experimental.pallas import tpu as pltpu
from jax.sharding import PartitionSpec as P

HEAD_DIM = 64
PIXEL_BLOCK = 8
LANES = 128
F32 = jnp.float32
BF16 = jnp.bfloat16
VMEM_BYTES = 50 * 1024 * 1024
MESH = pl.DeviceIdType.MESH


def call(body, out_shape, args, scratch=(), flops=0, **params):
    size = sum(a.size * a.dtype.itemsize for a in args)
    return pl.pallas_call(
        body,
        out_shape=out_shape,
        in_specs=[pl.BlockSpec(memory_space=pltpu.VMEM)] * len(args),
        out_specs=jax.tree.map(lambda _: pl.BlockSpec(memory_space=pltpu.VMEM), out_shape),
        scratch_shapes=list(scratch),
        compiler_params=pltpu.CompilerParams(vmem_limit_bytes=VMEM_BYTES, **params),
        cost_estimate=pl.CostEstimate(flops=flops, bytes_accessed=2 * size, transcendentals=0),
    )(*args)


def shape_of(shape, dtype):
    return jax.ShapeDtypeStruct(shape, dtype)


def dot(left, right, dims=((1,), (0,))):
    return lax.dot_general(left, right, (dims, ((), ())), preferred_element_type=F32)


def shifted(arr, step, rows, cols, pad):
    chans = arr.shape[-1]
    edge = 7 if step < 0 else cols + 8
    pad[:, edge : edge + 1] = jnp.zeros((rows, 1, chans), F32)
    pad[:, 8 : cols + 8] = arr.reshape(rows, cols, chans)
    return pad[:, 8 + step : 8 + step + cols].reshape(rows * cols, chans)


def conv_frame(f, top_ref, cells_ref, bottom_ref, weight_ref, ext, pad):
    frames, rows, cols, chans = cells_ref.shape
    ext[0] = top_ref[f]
    ext[1 : rows + 1] = cells_ref[f]
    ext[rows + 1] = bottom_ref[f]
    total = cells_ref[f].reshape(rows * cols, chans).astype(F32)
    for b in range(3):
        part = None
        for a in range(3):
            piece = ext[a : a + rows].reshape(rows * cols, chans)
            prod = dot(piece, weight_ref[3 * a + b])
            part = prod if part is None else part + prod
        total = total + (part if b == 1 else shifted(part, b - 1, rows, cols, pad))
    return total


def conv_scratch(rows, cols, chans):
    return [pltpu.VMEM((rows + 2, cols, chans), BF16), pltpu.VMEM((rows, cols + 16, chans), F32)]


def regroup(parts, groups):
    chans = parts[0].shape[-1]
    cat = jnp.concatenate([part.reshape(-1, PIXEL_BLOCK, chans) for part in parts], axis=1)
    return cat.astype(BF16)


def fill(out_ref, cells, start):
    count = min(out_ref.shape[0], cells.shape[0] - start)
    if count > 0:
        out_ref[0:count] = cells[start : start + count]
    if out_ref.shape[0] > count:
        out_ref[count:] = jnp.zeros((out_ref.shape[0] - count,) + out_ref.shape[1:], BF16)


def regroup_kernel(halves, cells_ref, out_ref):
    frames, rows, cols, chans = cells_ref.shape
    real = rows * cols // PIXEL_BLOCK
    parts = [cells_ref[f].reshape(rows * cols, chans).astype(F32) for f in range(frames)]
    cells = regroup(parts, real)
    per = sum(halves)
    owners = out_ref.shape[0] // per
    first = halves[0] * owners
    for owner in range(owners):
        at = owner * per
        for start, length, base in (
            (owner * halves[0], halves[0], 0),
            (first + owner * halves[1], halves[1], halves[0]),
        ):
            fill(out_ref.at[at + base : at + base + length], cells, min(start, real))


def conv_kernel(top_ref, cells_ref, bottom_ref, weight_ref, one_ref, two_ref, ext, pad, held):
    frames, rows, cols, chans = cells_ref.shape

    def one_frame(f, carry):
        held[f] = conv_frame(f, top_ref, cells_ref, bottom_ref, weight_ref, ext, pad)
        return carry

    lax.fori_loop(0, frames, one_frame, 0)
    real = rows * cols // PIXEL_BLOCK
    cells = regroup([held[f] for f in range(frames)], real)
    fill(one_ref, cells, 0)
    fill(two_ref, cells, one_ref.shape[0])


def convolve(top, cells, bottom, weight, counts):
    frames, rows, cols, chans = cells.shape
    return call(
        conv_kernel,
        tuple(shape_of((count, frames * PIXEL_BLOCK, chans), BF16) for count in counts),
        (top, cells, bottom, weight),
        conv_scratch(rows, cols, chans) + [pltpu.VMEM((frames, rows * cols, chans), F32)],
        flops=18 * cells.size * chans,
    )


def attend_kernel(
    base, hid, cot, wq, wk, wv, wot, wqt, wkt, wvt, cols_o, att_o, qg_o, kg_o, vg_o, q_s, k_s, v_s, g_s
):
    sources, groups, span, chans = hid.shape
    heads = chans // HEAD_DIM
    scale = HEAD_DIM ** (-0.5)
    size = sources * span
    flat = groups * span

    def project(t, carry):
        h = hid[t].reshape(flat, chans)
        for ref, w in ((q_s, wq), (k_s, wk), (v_s, wv)):
            ref[t] = dot(h, w[...]).astype(BF16).reshape(groups, span, chans)
        c = cot[t, base : base + groups].reshape(flat, chans)
        g_s[t] = dot(c, wot[...]).astype(BF16).reshape(groups, span, chans)
        return carry

    lax.fori_loop(0, sources, project, 0)

    place = lax.broadcasted_iota(jnp.int32, (1, chans), 1)
    head_masks = [
        jnp.where((place >= h * HEAD_DIM) & (place < (h + 1) * HEAD_DIM), 1.0, 0.0).astype(BF16)
        for h in range(heads)
    ]
    left = lax.broadcasted_iota(jnp.int32, (size, size), 0)
    right = lax.broadcasted_iota(jnp.int32, (size, size), 1)
    same = (left & (PIXEL_BLOCK - 1)) == (right & (PIXEL_BLOCK - 1))

    def one_group(g, carry):
        def get(ref):
            return ref[:, g].reshape(size, chans)

        def stack(arr):
            return jnp.concatenate([arr * m for m in head_masks], axis=0)

        q, k, v, og = get(q_s), get(k_s), get(v_s), get(g_s)
        kst, vst = stack(k), stack(v)
        scores = dot(q, kst, ((1,), (1,))) * scale
        dprobs = dot(og, vst, ((1,), (1,)))
        lows, lows_t, grads, grads_t = [], [], [], []
        for h in range(heads):
            block = slice(h * size, (h + 1) * size)
            s = jnp.where(same, scores[:, block], -1e30)
            e = jnp.exp(s - jnp.max(s, axis=1, keepdims=True))
            prob = e / jnp.sum(e, axis=1, keepdims=True)
            dp = dprobs[:, block]
            ds = prob * (dp - jnp.sum(prob * dp, axis=1, keepdims=True)) * scale
            low, grad = prob.astype(BF16), ds.astype(BF16)
            lows.append(low)
            grads.append(grad)
            lows_t.append(low.T)
            grads_t.append(grad.T)
        shape = (sources, span, chans)
        low = jnp.concatenate(lows, axis=1)
        grad = jnp.concatenate(grads, axis=1)
        low_t = jnp.concatenate(lows_t, axis=1)
        grad_t = jnp.concatenate(grads_t, axis=1)
        att_o[:, g] = dot(low, vst).astype(BF16).reshape(shape)
        qg_o[:, g] = dot(grad, kst).astype(BF16).reshape(shape)
        kg_o[:, g] = dot(grad_t, stack(q)).astype(BF16).reshape(shape)
        vg_o[:, g] = dot(low_t, stack(og)).astype(BF16).reshape(shape)
        return carry

    lax.fori_loop(0, groups, one_group, 0)

    def back(t, carry):
        total = dot(qg_o[t].reshape(flat, chans), wqt[...])
        total = total + dot(kg_o[t].reshape(flat, chans), wkt[...])
        total = total + dot(vg_o[t].reshape(flat, chans), wvt[...])
        cols_o[t] = total.astype(BF16).reshape(groups, span, chans)
        return carry

    lax.fori_loop(0, sources, back, 0)


def pack_places(count, chans):
    whole, rest = chans // LANES, chans % LANES
    places, row = [], 0
    for m in range(count):
        for block in range(whole):
            places.append((row, 0, m, block * LANES, LANES))
            row += chans
    lane = 0
    for m in range(count if rest else 0):
        places.append((row, lane, m, whole * LANES, rest))
        lane += rest
        if lane + rest > LANES:
            row, lane = row + chans, 0
    return places, row + (chans if lane else 0)


def pack(total, out_ref):
    count, chans, _ = total.shape
    places, used = pack_places(count, chans)
    out_ref[used:] = jnp.zeros((out_ref.shape[0] - used, LANES), F32)
    if places[-1][1] + places[-1][4] < LANES:
        out_ref[used - chans : used] = jnp.zeros((chans, LANES), F32)
    for row, lane, m, col, width in places:
        out_ref[row : row + chans, lane : lane + width] = total[m, :, col : col + width]


def part_size(count, chans, parts, devices):
    unit = parts * devices * 16
    return -(-pack_places(count, chans)[1] // unit) * devices * 16


def weight_grads_kernel(cot, *refs):
    halves, total = (refs[0:5], refs[5:10]), refs[10]
    total[...] = jnp.zeros(total.shape, F32)

    def one(t, carry):
        base = 0
        for hid, att, qg, kg, vg in halves:
            _, groups, span, chans = hid.shape
            flat = groups * span
            ht = hid[t].reshape(flat, chans).T
            for i, ref in enumerate((qg, kg, vg)):
                total[i] += dot(ht, ref[t].reshape(flat, chans))
            c = cot[t, base : base + groups].reshape(flat, chans)
            total[3] += dot(att[t].reshape(flat, chans).T, c)
            base += groups
        return carry

    lax.fori_loop(0, cot.shape[0], one, 0)


def hidden_grad_kernel(one_ref, two_ref, cot_ref, out_ref, first_ref, last_ref):
    frames, rows, cols, chans = cot_ref.shape
    real = rows * cols // PIXEL_BLOCK
    rest = real - one_ref.shape[0]
    back = jnp.concatenate([one_ref[...].astype(F32), two_ref[0:rest].astype(F32)], axis=0)
    for f in range(frames):
        piece = back[:, f * PIXEL_BLOCK : (f + 1) * PIXEL_BLOCK].reshape(rows, cols, chans)
        total = (cot_ref[f].astype(F32) + piece).astype(BF16)
        out_ref[f] = total
        first_ref[f] = total[0]
        last_ref[f] = total[rows - 1]


def conv_grad_kernel(top_ref, cells_ref, bottom_ref, grad_ref, others_ref, out_ref, ext, pad, total):
    frames, rows, cols, chans = cells_ref.shape
    total[0:9] = jnp.zeros((9,) + total.shape[1:], F32)
    total[9:] = others_ref[...]

    def one_frame(f, carry):
        ext[0] = top_ref[f]
        ext[1 : rows + 1] = cells_ref[f]
        ext[rows + 1] = bottom_ref[f]
        grad = grad_ref[f].reshape(rows * cols, chans)
        wide = grad.astype(F32)
        moved = [
            shifted(wide, 1, rows, cols, pad).astype(BF16),
            grad,
            shifted(wide, -1, rows, cols, pad).astype(BF16),
        ]
        for a in range(3):
            turned = ext[a : a + rows].reshape(rows * cols, chans).T
            for b in range(3):
                total[3 * a + b] += dot(turned, moved[b])
        return carry

    lax.fori_loop(0, frames, one_frame, 0)
    pack(total, out_ref)


def hops(sizes, parts):
    space, tm = sizes
    first, planes, line = [("space", 1)], [], []
    stride = 2
    while stride < space:
        planes.append(("space", stride))
        stride *= 2
    stride = 1
    while stride < tm:
        line.append(("tm", stride))
        stride *= 2
    rest = planes + line
    plan = [first + rest[p:] + rest[:p] for p in range(parts)]
    return plan, first + planes + line


def reduce_kernel(plan, greet, part_rows, *refs):
    x_ref, top_ref, cells_ref, bottom_ref, weight_ref, out_ref, result_ref = refs[:7]
    ext, pad, acc, low, send_sems, recv_sems, *recvs = refs[7:]
    frames, rows, cols, chans = cells_ref.shape

    def bit_and_partner(axis, stride):
        me = lax.axis_index(axis)
        bit = (me // stride) % 2
        return bit, me + (1 - 2 * bit) * stride

    barrier = pltpu.get_barrier_semaphore()
    for axis, stride in greet:
        _, partner = bit_and_partner(axis, stride)
        pl.semaphore_signal(barrier, inc=1, device_id={axis: partner}, device_id_type=MESH)
    pl.semaphore_wait(barrier, len(greet))

    parts, steps = len(plan), len(plan[0])
    offs = [p * part_rows for p in range(parts)]
    size = part_rows
    for s in range(steps):
        half = size // 2
        src = x_ref if s == 0 else acc
        copies, keeps = [], []
        for p in range(parts):
            axis, stride = plan[p][s]
            bit, partner = bit_and_partner(axis, stride)
            send = pl.multiple_of(offs[p] + (1 - bit) * half, 16)
            keeps.append(pl.multiple_of(offs[p] + bit * half, 16))
            copy = pltpu.make_async_remote_copy(
                src_ref=src.at[pl.ds(send, half)],
                dst_ref=recvs[s].at[p],
                send_sem=send_sems.at[s, p],
                recv_sem=recv_sems.at[s, p],
                device_id={axis: partner},
                device_id_type=MESH,
            )
            copy.start()
            copies.append(copy)
        for f in range(s, frames, steps):
            total = conv_frame(f, top_ref, cells_ref, bottom_ref, weight_ref, ext, pad)
            result_ref[f] = total.astype(BF16).reshape(rows, cols, chans)
        for p in range(parts):
            copies[p].wait()
            acc[pl.ds(keeps[p], half)] = src[pl.ds(keeps[p], half)] + recvs[s][p]
        offs, size = keeps, half
    for p in range(parts):
        low[pl.ds(offs[p], size)] = acc[pl.ds(offs[p], size)].astype(BF16)
    for s in range(steps - 1, -1, -1):
        copies, wider = [], []
        for p in range(parts):
            axis, stride = plan[p][s]
            bit, partner = bit_and_partner(axis, stride)
            mine = low.at[pl.ds(offs[p], size)]
            copy = pltpu.make_async_remote_copy(
                src_ref=mine,
                dst_ref=mine,
                send_sem=send_sems.at[steps + s, p],
                recv_sem=recv_sems.at[steps + s, p],
                device_id={axis: partner},
                device_id_type=MESH,
            )
            copy.start()
            copies.append(copy)
            wider.append(pl.multiple_of(offs[p] - bit * size, 16))
        for copy in copies:
            copy.wait()
        offs, size = wider, size * 2
    out_ref[...] = low[...]


def unpack_kernel(norm, packed_ref, conv_ref, *refs):
    chans = conv_ref.shape[-1]
    taps = conv_ref.shape[0]
    for row, lane, m, col, width in pack_places(taps + len(refs), chans)[0]:
        piece = packed_ref[row : row + chans, lane : lane + width].astype(F32) * norm
        if m < taps:
            conv_ref[m, :, col : col + width] = piece
        else:
            refs[m - taps][:, col : col + width] = piece


def total_over_devices(arr, chans, norm, sizes, parts, part_rows, conv):
    plan, greet = hops(sizes, parts)
    steps = len(greet)
    out = (shape_of(arr.shape, BF16), shape_of(conv[1].shape, BF16))
    scratch = conv_scratch(*conv[1].shape[1:])
    scratch += [
        pltpu.VMEM(arr.shape, F32),
        pltpu.VMEM(arr.shape, BF16),
        pltpu.SemaphoreType.DMA((2 * steps, parts)),
        pltpu.SemaphoreType.DMA((2 * steps, parts)),
    ]
    scratch += [pltpu.VMEM((parts, part_rows >> (s + 1), LANES), F32) for s in range(steps)]
    packed, result = call(
        functools.partial(reduce_kernel, plan, greet, part_rows),
        out,
        (arr,) + conv,
        scratch,
        collective_id=0,
        has_side_effects=True,
    )
    grads = call(
        functools.partial(unpack_kernel, norm),
        (shape_of((9, chans, chans), F32),) + (shape_of((chans, chans), F32),) * 4,
        (packed,),
    )
    return grads, result


def halo(first, last):
    count = lax.axis_size("space")
    up = [(i, i + 1) for i in range(count - 1)]
    down = [(i + 1, i) for i in range(count - 1)]
    return lax.ppermute(last, "space", up), lax.ppermute(first, "space", down)


def on_device(latents, cotangent, conv_weight, query_weight, key_weight, value_weight, out_weight):
    frames, rows, cols, chans = latents.shape
    sizes = (lax.axis_size("space"), lax.axis_size("tm"))
    space, tm = sizes
    whole_count = frames * tm * rows * space * cols
    norm = float(whole_count) ** -0.5
    devices = space * tm
    per_source = -(-(rows * cols // PIXEL_BLOCK) // tm)
    groups = per_source * tm
    span = frames * PIXEL_BLOCK
    halves = (-(-per_source // 2), per_source // 2)

    def exchange(arr):
        return lax.all_to_all(arr, "tm", split_axis=0, concat_axis=0, tiled=True)

    def owned(arr, count):
        return exchange(arr).reshape(tm, count, span, chans)

    top, bottom = halo(latents[:, 0], latents[:, rows - 1])
    cot_groups = call(
        functools.partial(regroup_kernel, halves),
        shape_of((groups, span, chans), BF16),
        (cotangent,),
    )
    cot_all = owned(cot_groups, per_source)
    weights = conv_weight.reshape(9, chans, chans)
    hidden = convolve(top, latents, bottom, weights, [tm * half for half in halves])
    hidden, cot_all = lax.optimization_barrier((hidden, cot_all))
    backs, saved = [], []
    for i, half in enumerate(halves):
        hid = owned(hidden[i], half)
        tile = shape_of(hid.shape, BF16)
        attn_cols, *grads = call(
            functools.partial(attend_kernel, i * halves[0]),
            (tile,) * 5,
            (
                hid,
                cot_all,
                query_weight,
                key_weight,
                value_weight,
                out_weight.T,
                query_weight.T,
                key_weight.T,
                value_weight.T,
            ),
            [pltpu.VMEM(hid.shape, BF16)] * 4,
            flops=20 * hid.size * chans,
        )
        backs.append(exchange(attn_cols.reshape(tm * half, span, chans)))
        saved += [hid] + grads
    small = call(
        weight_grads_kernel,
        shape_of((4, chans, chans), F32),
        (cot_all, *saved),
        flops=8 * cot_all.size * chans,
    )
    hidden_grad, first, last = call(
        hidden_grad_kernel,
        (
            shape_of(latents.shape, BF16),
            shape_of((frames, cols, chans), BF16),
            shape_of((frames, cols, chans), BF16),
        ),
        (*backs, cotangent),
    )
    grad_top, grad_bottom = halo(first, last)
    part_rows = part_size(13, chans, 3, devices)
    packed = call(
        conv_grad_kernel,
        shape_of((3 * part_rows, LANES), F32),
        (top, latents, bottom, hidden_grad, small),
        conv_scratch(rows, cols, chans) + [pltpu.VMEM((13, chans, chans), F32)],
        flops=18 * latents.size * chans,
    )
    turned = jnp.swapaxes(conv_weight[::-1, ::-1], 2, 3).reshape(9, chans, chans)
    (grad_conv, *others), grad_input = total_over_devices(
        packed,
        chans,
        norm,
        sizes,
        3,
        part_rows,
        (grad_top, hidden_grad, grad_bottom, turned),
    )
    return grad_input, grad_conv.reshape(3, 3, chans, chans), *others


def solution(mesh):
    in_specs = (P("tm", "space", None, None), P("tm", "space", None, None), P(), P(), P(), P(), P())
    out_specs = (P("tm", "space", None, None), P(), P(), P(), P(), P())
    return jax.shard_map(
        on_device, mesh=mesh, in_specs=in_specs, out_specs=out_specs, check_vma=False
    )
```
